32 devices in a mesh: trow: 4 (over x, core), tcol: 4 (over z), visit: 2 (over y).
Axes of the slice: x: 2, y: 2, z: 4, core: 2. Of those that a mesh axis runs over, the one named last changes fastest.
Arguments:
- template: float32 [2048, 2048], P(('trow', 'visit'), 'tcol'), may hold values from -6 to 6
- warped: float32 [384, 256, 256], P(('trow', 'tcol', 'visit')), may hold values from -6 to 6
- coeffs: float32 [384, 27, 3], P(('trow', 'tcol', 'visit')), may hold values from -2 to 2
- dest_tile: int32 [384, 1], P(('trow', 'tcol', 'visit')), may hold values from 0 to 15; in each aligned block of 12 rows (0 to 11, 12 to 23, ...) at most 2 rows name the same one
- position: int32 [384, 1], P(('trow', 'tcol', 'visit')), may hold values from 0 to 3
Outputs:
- difference: float32 [384, 256, 256], P(('trow', 'tcol', 'visit'))
The draws below stay inside these ranges and needn't reach their ends.
Inputs may be any that keep to these rules, and one draw needn't show every extreme that they name: `dest_tile`: tile index = tract row times the number of tract columns plus tract column; among the 12 blocks of one device no tile is named more than 2 times. `position`: sub-block row times 512 / 256 plus sub-block column.
All inputs are finite; a program needn't handle non-finite values.
Results may differ from the reference program's by a relative error of at most 0.0003.
Values sent between devices are 32-bit elements; how exact they have to be, the bound alone decides.
A program may use at most 192 MiB of HBM per device.

```python
import math
import jax
import jax.numpy as jnp
import numpy as np
from jax import lax

TILE = 512
BLK = 256
HALF = 10
NB = 12
CAP = 2
NR = 2048
NC = 2048
BLOCKS = 384
N_TROW = 4
N_TCOL = 4


def set_ends(values, stream_key, low, largest):
    extent = values.shape
    index_at = [jax.random.randint(jax.random.fold_in(stream_key, axis), (), 0, extent[axis]) for axis in range(len(extent))]
    values = values.at[tuple(index_at)].set(low)
    longest = extent.index(max(extent))
    index_at[longest] = (index_at[longest] + 1) % extent[longest]
    return values.at[tuple(index_at)].set(largest)


def block_levels(key, dims, cuts, smallest, largest):
    def one(axis_at, shards_of):
        steps = jax.random.uniform(jax.random.fold_in(jax.random.fold_in(key, 6), axis_at), (shards_of,), jnp.float32, smallest / len(cuts), largest / len(cuts))
        return jnp.repeat(jnp.exp(steps), dims[axis_at] // shards_of).reshape((-1,) + (1,) * (len(dims) - axis_at - 1))

    factor_of = one(*cuts[0])
    for cut in cuts[1:]:
        factor_of = factor_of * one(*cut)
    return factor_of


def assign_block(key, own, number, rows, number_of, top, limit, slope):
    sequence = jax.random.permutation(key, number_of)
    crowded, common = load_shares(number_of, rows * top, limit, slope, True), load_shares(number_of, rows * top, limit, slope, False)
    places = jnp.arange(number_of)

    def named(lengths, offset_by):
        used = int((lengths > 0).sum())
        fixed = max(1, used // 4)
        moved = fixed + (places - fixed + offset_by * (used - fixed)) % max(1, number_of - fixed)
        return jnp.zeros((number_of,), jnp.int32).at[sequence[jnp.where(places < fixed, places, moved)]].set(jnp.asarray(lengths, jnp.int32))

    lengths = jnp.where(number % 4 == 0, named(crowded, number // 4), named(common, number - number // 4 - 1))
    mixed = jax.random.permutation(jax.random.fold_in(own, 3), number_of)
    source_of, receiver = mixed[0:number_of // 2 * 2:2], mixed[1:number_of // 2 * 2:2]
    slack = jnp.minimum(lengths[source_of] - 1, limit - lengths[receiver]) // 2
    slack = jnp.where((source_of == sequence[0]) | (receiver == sequence[0]) | (lengths[receiver] == 0), 0, jnp.maximum(slack, 0))
    moved = jax.random.randint(jax.random.fold_in(own, 4), (number_of // 2,), 0, 1 << 20) % (slack + 1)
    lengths = lengths.at[source_of].add(-moved).at[receiver].add(moved)
    items = jnp.searchsorted(jnp.cumsum(lengths), jnp.arange(rows * top), side="right").astype(jnp.int32)
    listing = items.reshape(top, rows).T
    listing = listing[jax.random.permutation(jax.random.fold_in(own, 1), rows)]
    offset_by = jax.random.randint(jax.random.fold_in(own, 2), (rows, 1), 0, top)
    return jnp.take_along_axis(listing, (jnp.arange(top)[None, :] + offset_by) % top, axis=1)


def load_shares(number_of, total, bound, lean, full):
    weights = [(1 << 20) // math.isqrt(standing ** lean) + 1 for standing in range(1, number_of + 1)]
    largest = bound if full else min(bound, max(-(-total // number_of), total * weights[0] // sum(weights)))
    least = 1 if total - largest >= number_of - 1 else 0
    counts, surplus = [largest] + [least] * (number_of - 1), total - largest - least * (number_of - 1)
    while surplus > 0:
        free = [i for i in range(1, number_of) if counts[i] < largest] or [i for i in range(1, number_of) if counts[i] < bound]
        pool, remaining = sum([weights[i] for i in free]), surplus
        for i in free:
            addition = min(bound - counts[i], max(1, remaining * weights[i] // pool), surplus)
            counts[i] = counts[i] + addition
            surplus = surplus - addition
    return np.array(counts)


def bell_draw(key, shape, deviation, reach, cuts=(), kind=jnp.bfloat16):
    level = block_levels(key, shape, cuts, -0.22, 0.18) if cuts else 1.0
    entries = jax.random.normal(key, shape, jnp.float32) * deviation * level
    return jnp.minimum(jnp.maximum(entries, -reach), reach).astype(kind)


def setup_inputs(seed: int = 0) -> dict:
    key_of = jax.random.split(jax.random.key(seed), 6)
    template = bell_draw(key_of[0], (NR, NC), 1.0, 6.0, ((0, 8), (1, 4)), jnp.float32)
    warped = bell_draw(key_of[1], (BLOCKS, BLK, BLK), 1.0, 6.0, ((0, 32),), jnp.float32)
    coeffs = bell_draw(key_of[2], (BLOCKS, 27, 3), 0.25, 2.0, ((0, 32),), jnp.float32)
    dest_tile_keys = jax.random.split(jax.random.fold_in(key_of[3], 1), BLOCKS // NB)
    dest_tile_turns = jax.random.permutation(jax.random.fold_in(key_of[3], 3), BLOCKS // NB)
    dest_tile = jax.vmap(lambda own, number: assign_block(jax.random.fold_in(key_of[3], 2), own, number, NB, N_TROW * N_TCOL, 1, CAP, 2))(dest_tile_keys, dest_tile_turns).reshape((BLOCKS, 1))
    position = set_ends(jax.random.randint(key_of[4], (BLOCKS, 1), 0, (TILE // BLK) * (TILE // BLK)), jax.random.fold_in(key_of[4], 1), 0, ((TILE // BLK) * (TILE // BLK)) - 1).astype(jnp.int32)
    return dict(template=template, warped=warped, coeffs=coeffs, dest_tile=dest_tile, position=position)


SPREADS = (1.0, 2.0, 4.0)
DEGREES = (4, 2, 2)

def taps_for(spread, power):
    offsets = jnp.arange(-HALF, HALF + 1).astype(jnp.float32)
    weights = jnp.exp(-offsets * offsets / (2.0 * spread * spread))
    for step in range(power):
        weights = weights * offsets
    return weights / jnp.sqrt(jnp.sum(weights * weights))

def band_matrix(tap_weights, length):
    row_ids = jnp.arange(length)[:, None]
    col_ids = jnp.arange(length + 2 * HALF)[None, :]
    offset = col_ids - row_ids
    matrix = jnp.zeros((length, length + 2 * HALF), jnp.float32)
    for tap_index in range(2 * HALF + 1):
        matrix = matrix + jnp.where(offset == tap_index, tap_weights[tap_index], 0.0)
    return matrix

def basis_images(window, out_rows, out_cols):
    highest = lax.Precision.HIGHEST
    stacked = []
    for spread, degree in zip(SPREADS, DEGREES):
        row_passes = [jnp.dot(band_matrix(taps_for(spread, power), out_rows), window, precision=highest) for power in range(degree + 1)]
        col_bands = [band_matrix(taps_for(spread, power), out_cols) for power in range(degree + 1)]
        for row_power in range(degree + 1):
            for col_power in range(degree + 1 - row_power):
                stacked.append(jnp.dot(row_passes[row_power], col_bands[col_power].T, precision=highest))
    return jnp.stack(stacked)

def block_model(images, coef_block, row_start, col_start):
    zero = jnp.int32(0)
    piece = lax.dynamic_slice(images, (zero, row_start.astype(jnp.int32), col_start.astype(jnp.int32)), (images.shape[0], BLK, BLK))
    mixed = jnp.einsum('bj,bxy->jxy', coef_block, piece, precision=lax.Precision.HIGHEST)
    coords = (jnp.arange(BLK).astype(jnp.float32) - (BLK - 1) / 2.0) / ((BLK - 1) / 2.0)
    return mixed[0] + coords[None, :] * mixed[1] + coords[:, None] * mixed[2]

def reference(template, warped, coeffs, dest_tile, position):
    padded = jnp.pad(template, HALF)
    subs = TILE // BLK

    def tile_images(tile_index):
        row_tile = tile_index // N_TCOL
        col_tile = tile_index % N_TCOL
        window = lax.dynamic_slice(padded, ((row_tile * TILE).astype(jnp.int32), (col_tile * TILE).astype(jnp.int32)), (TILE + 2 * HALF, TILE + 2 * HALF))
        return basis_images(window, TILE, TILE)
    images_all = lax.map(tile_images, jnp.arange(N_TROW * N_TCOL, dtype=jnp.int32))

    def block_difference(packed):
        image_block, coef_block, tile_id, sub_place = packed
        images = lax.dynamic_index_in_dim(images_all, tile_id.astype(jnp.int32), 0, keepdims=False)
        model = block_model(images, coef_block, sub_place // subs * BLK, sub_place % subs * BLK)
        return image_block - model
    return lax.map(block_difference, (warped, coeffs, dest_tile[:, 0], position[:, 0]))
```

```python
import jax
import jax.numpy as jnp
import numpy as np
from jax import lax
from jax.experimental import pallas as pl
from jax.experimental.pallas import tpu as pltpu
from jax.sharding import PartitionSpec as P

BLK = 256
HALF = 10
SPREADS = (1.0, 2.0, 4.0)
DEGREES = (4, 2, 2)
STRIP = 128
EDGE = 16
SPAN = STRIP + 2 * EDGE
LANE = 128
FILTERS = [(s, k) for s in range(3) for k in range(DEGREES[s] + 1)]
DEPTH = -(-len(FILTERS) * SPAN // 256) * 256
POWERS = max(DEGREES) + 1


def taps():
    offsets = np.arange(-HALF, HALF + 1).astype(np.float64)
    table = {}
    for s, spread in enumerate(SPREADS):
        for k in range(DEGREES[s] + 1):
            weights = offsets**k * np.exp(-offsets * offsets / (2.0 * spread * spread))
            table[s, k] = weights / np.sqrt(np.sum(weights * weights))
    return table


def split(values):
    high = values.astype(jnp.bfloat16)
    return high, (values - high.astype(jnp.float32)).astype(jnp.bfloat16)


def constants():
    table = taps()
    index = {}
    for s, degree in enumerate(DEGREES):
        for i in range(degree + 1):
            for j in range(degree + 1 - i):
                index[s, i, j] = len(index)
    columns = np.zeros((2 * STRIP, len(FILTERS) * STRIP), np.float32)
    rows = np.zeros((POWERS, STRIP, DEPTH), np.float32)
    spread_out = np.zeros((len(index), POWERS, DEPTH), np.float32)
    for f, (s, k) in enumerate(FILTERS):
        for y in range(STRIP):
            columns[y : y + 2 * HALF + 1, f * STRIP + y] = table[s, k]
        for i in range(DEGREES[s] + 1 - k):
            spread_out[index[s, i, k], i, f * SPAN : (f + 1) * SPAN] = 1.0
            for x in range(STRIP):
                start = f * SPAN + x + EDGE - HALF
                rows[i, x, start : start + 2 * HALF + 1] = table[s, i]
    return columns, rows, spread_out.reshape(len(index), -1)


def mixing_kernel(coef_ref, rows_ref, out_ref):
    def mixed(q, lo, hi):
        total = None
        for i in range(POWERS):
            used = [f for f, (s, k) in enumerate(FILTERS) if i + k <= DEGREES[s]]
            if not any(f * SPAN < hi and (f + 1) * SPAN > lo for f in used):
                continue
            term = coef_ref[0, q : q + 1, i * DEPTH + lo : i * DEPTH + hi] * rows_ref[i, :, lo:hi]
            total = term if total is None else total + term
        return total

    place = lax.broadcasted_iota(jnp.int32, (STRIP, 1), 0).astype(jnp.float32)
    middle = (BLK - 1) / 2.0
    for lo in range(0, DEPTH, 256):
        hi = lo + 256
        flat, across, down = mixed(0, lo, hi), mixed(1, lo, hi), mixed(2, lo, hi)
        parts = [flat + (place + (STRIP * t - middle)) / middle * down for t in range(2)] + [across]
        for p, part in enumerate(parts):
            high, low = split(part)
            out_ref[0, p, 0, :, lo:hi] = high
            out_ref[0, p, 1, :, lo:hi] = low


def mixing(expanded, rows):
    blocks = expanded.shape[0]
    return pl.pallas_call(
        mixing_kernel,
        grid=(blocks,),
        in_specs=[
            pl.BlockSpec((1, 3, POWERS * DEPTH), lambda n: (n, 0, 0)),
            pl.BlockSpec((POWERS, STRIP, DEPTH), lambda n: (0, 0, 0)),
        ],
        out_specs=pl.BlockSpec((1, 3, 2, STRIP, DEPTH), lambda n: (n, 0, 0, 0, 0)),
        out_shape=jax.ShapeDtypeStruct((blocks, 3, 2, STRIP, DEPTH), jnp.bfloat16),
        compiler_params=pltpu.CompilerParams(vmem_limit_bytes=40 << 20),
        cost_estimate=pl.CostEstimate(
            flops=blocks * 40 * STRIP * DEPTH, bytes_accessed=blocks * 14 * STRIP * DEPTH, transcendentals=0
        ),
        name="row_matrices",
    )(expanded, rows)


def model_kernel(row_tiles, col_tiles, subs, tile_ref, place_ref, mix_ref, warped_ref, chigh_ref, clow_ref,
                 sky_ref, out_ref, window, bhigh, blow, sems):
    step = pl.program_id(0)
    steps = pl.num_programs(0)
    tile_rows = subs * BLK

    def corner(n):
        tile, place = tile_ref[n], place_ref[n]
        return (tile // col_tiles) * subs + place // subs, (tile % col_tiles) * subs + place % subs

    def copies(n, slot):
        a, b = corner(n)
        found = []
        for dr, (from_row, to_row, height) in enumerate(((BLK - EDGE, 0, EDGE), (0, EDGE, BLK), (0, EDGE + BLK, EDGE))):
            for dc, (from_col, to_col, width) in enumerate(((BLK - LANE, 0, LANE), (0, LANE, BLK), (0, LANE + BLK, LANE))):
                ra = jnp.clip(a + dr - 1, 0, row_tiles * subs - 1)
                cb = jnp.clip(b + dc - 1, 0, col_tiles * subs - 1)
                row = ((ra // subs) * col_tiles + cb // subs) * tile_rows + (ra % subs) * BLK + from_row
                col = (cb % subs) * BLK + from_col
                found.append(
                    pltpu.make_async_copy(
                        sky_ref.at[pl.ds(pl.multiple_of(row, EDGE), height), pl.ds(pl.multiple_of(col, LANE), width)],
                        window.at[slot, pl.ds(to_row, height), pl.ds(to_col, width)],
                        sems.at[slot, dr * 3 + dc],
                    )
                )
        return found

    @pl.when(step == 0)
    def _():
        used = len(FILTERS) * SPAN
        for t in range(2):
            bhigh[t, used:, :] = jnp.zeros((DEPTH - used, BLK), jnp.bfloat16)
            blow[t, used:, :] = jnp.zeros((DEPTH - used, BLK), jnp.bfloat16)
        for copy in copies(0, 0):
            copy.start()

    slot = lax.rem(step, 2)

    @pl.when(step + 1 < steps)
    def _():
        for copy in copies(step + 1, 1 - slot):
            copy.start()

    for copy in copies(step, slot):
        copy.wait()

    a, b = corner(step)
    rows_all, cols_all = BLK + 2 * EDGE, BLK + 2 * LANE

    @pl.when(a == 0)
    def _():
        window[slot, :EDGE, :] = jnp.zeros((EDGE, cols_all), jnp.float32)

    @pl.when(a == row_tiles * subs - 1)
    def _():
        window[slot, EDGE + BLK :, :] = jnp.zeros((EDGE, cols_all), jnp.float32)

    @pl.when(b == 0)
    def _():
        window[slot, :, :LANE] = jnp.zeros((rows_all, LANE), jnp.float32)

    @pl.when(b == col_tiles * subs - 1)
    def _():
        window[slot, :, LANE + BLK :] = jnp.zeros((rows_all, LANE), jnp.float32)

    dot = lambda x, y: jnp.dot(x, y, preferred_element_type=jnp.float32)
    shifted = pltpu.roll(window[slot], cols_all - (LANE - HALF), 1)
    high, low = split(shifted)
    high = jnp.concatenate([high[:, :BLK], high[:, STRIP : STRIP + BLK]], axis=0)
    low = jnp.concatenate([low[:, :BLK], low[:, STRIP : STRIP + BLK]], axis=0)
    for lo in range(0, len(FILTERS), 2):
        count = min(2, len(FILTERS) - lo)
        lanes = slice(lo * STRIP, (lo + count) * STRIP)
        chigh = chigh_ref[:, lanes]
        product = dot(high, chigh) + dot(low, chigh) + dot(high, clow_ref[:, lanes])
        phigh, plow = split(product)
        for f in range(count):
            for yt in range(2):
                for xt in range(2):
                    start = yt * rows_all + xt * STRIP
                    source = (slice(start, start + SPAN), slice(f * STRIP, (f + 1) * STRIP))
                    target = (xt, slice((lo + f) * SPAN, (lo + f + 1) * SPAN), slice(yt * STRIP, (yt + 1) * STRIP))
                    bhigh[target] = phigh[source]
                    blow[target] = plow[source]

    middle = (BLK - 1) / 2.0
    across = (lax.broadcasted_iota(jnp.int32, (1, BLK), 1).astype(jnp.float32) - middle) / middle
    for t in range(2):
        mhigh = jnp.concatenate([mix_ref[0, t, 0], mix_ref[0, 2, 0]], axis=0)
        mlow = jnp.concatenate([mix_ref[0, t, 1], mix_ref[0, 2, 1]], axis=0)
        right = bhigh[t]
        both = dot(mhigh, right) + dot(mlow, right) + dot(mhigh, blow[t])
        model = both[:STRIP] + across * both[STRIP:]
        rows = slice(t * STRIP, (t + 1) * STRIP)
        out_ref[0, rows, :] = warped_ref[0, rows, :] - model


def differences(sky, mix, warped, dest, place, row_tiles, col_tiles, subs, chigh, clow):
    blocks = warped.shape[0]
    rows_all, cols_all = BLK + 2 * EDGE, BLK + 2 * LANE

    def kernel(*refs):
        model_kernel(row_tiles, col_tiles, subs, *refs)

    return pl.pallas_call(
        kernel,
        grid_spec=pltpu.PrefetchScalarGridSpec(
            num_scalar_prefetch=2,
            grid=(blocks,),
            in_specs=[
                pl.BlockSpec((1, 3, 2, STRIP, DEPTH), lambda n, *_: (n, 0, 0, 0, 0)),
                pl.BlockSpec((1, BLK, BLK), lambda n, *_: (n, 0, 0)),
                pl.BlockSpec(chigh.shape, lambda n, *_: (0, 0)),
                pl.BlockSpec(clow.shape, lambda n, *_: (0, 0)),
                pl.BlockSpec(memory_space=pl.ANY),
            ],
            out_specs=pl.BlockSpec((1, BLK, BLK), lambda n, *_: (n, 0, 0)),
            scratch_shapes=[
                pltpu.VMEM((2, rows_all, cols_all), jnp.float32),
                pltpu.VMEM((2, DEPTH, BLK), jnp.bfloat16),
                pltpu.VMEM((2, DEPTH, BLK), jnp.bfloat16),
                pltpu.SemaphoreType.DMA((2, 9)),
            ],
        ),
        out_shape=jax.ShapeDtypeStruct(warped.shape, jnp.float32),
        compiler_params=pltpu.CompilerParams(vmem_limit_bytes=48 << 20),
        cost_estimate=pl.CostEstimate(
            flops=blocks * 2900000000, bytes_accessed=blocks * 4000000, transcendentals=0
        ),
        name="differences",
    )(dest, place, mix, warped, chigh, clow, sky)


def local_part(sky, warped, coeffs, dest, place, row_tiles, col_tiles, subs):
    columns, rows, spread_out = constants()
    chigh = columns.astype(jnp.bfloat16)
    clow = (columns - chigh.astype(np.float32)).astype(jnp.bfloat16)
    expanded = jnp.einsum("nbq,bk->nqk", coeffs, spread_out, precision=lax.Precision.HIGHEST)
    mix = mixing(expanded, jnp.asarray(rows))
    return differences(
        sky, mix, warped, dest, place, row_tiles, col_tiles, subs, jnp.asarray(chigh), jnp.asarray(clow)
    )


def on_device(template, warped, coeffs, dest_tile, position):
    axes = ("trow", "tcol", "visit")
    sky = lax.all_gather(template, axes, axis=0, tiled=True)
    subs = template.shape[1] // BLK
    return local_part(
        sky, warped, coeffs, dest_tile[:, 0], position[:, 0],
        lax.axis_size("trow"), lax.axis_size("tcol"), subs,
    )


def solution(mesh):
    return jax.shard_map(
        on_device,
        mesh=mesh,
        in_specs=(
            P(("trow", "visit"), "tcol"),
            P(("trow", "tcol", "visit"), None, None),
            P(("trow", "tcol", "visit"), None, None),
            P(("trow", "tcol", "visit"), None),
            P(("trow", "tcol", "visit"), None),
        ),
        out_specs=P(("trow", "tcol", "visit"), None, None),
        check_vma=False,
    )
```

```python
import jax
import jax.numpy as jnp
import numpy as np
from jax import lax
from jax.experimental import pallas as pl
from jax.experimental.pallas import tpu as pltpu
from jax.sharding import PartitionSpec as P

BLK = 256
HALF = 10
SPREADS = (1.0, 2.0, 4.0)
DEGREES = (4, 2, 2)
STRIP = 128
EDGE = 16
SPAN = STRIP + 2 * EDGE
LANE = 128
FILTERS = [(s, k) for s in range(3) for k in range(DEGREES[s] + 1)]
DEPTH = -(-len(FILTERS) * SPAN // 256) * 256
POWERS = max(DEGREES) + 1


def taps():
    offsets = np.arange(-HALF, HALF + 1).astype(np.float64)
    table = {}
    for s, spread in enumerate(SPREADS):
        for k in range(DEGREES[s] + 1):
            weights = offsets**k * np.exp(-offsets * offsets / (2.0 * spread * spread))
            table[s, k] = weights / np.sqrt(np.sum(weights * weights))
    return table


def split(values):
    high = values.astype(jnp.bfloat16)
    return high, (values - high.astype(jnp.float32)).astype(jnp.bfloat16)


def constants():
    table = taps()
    index = {}
    for s, degree in enumerate(DEGREES):
        for i in range(degree + 1):
            for j in range(degree + 1 - i):
                index[s, i, j] = len(index)
    columns = np.zeros((2 * STRIP, len(FILTERS) * STRIP), np.float32)
    rows = np.zeros((POWERS, STRIP, DEPTH), np.float32)
    spread_out = np.zeros((len(index), POWERS, DEPTH), np.float32)
    for f, (s, k) in enumerate(FILTERS):
        for y in range(STRIP):
            columns[y : y + 2 * HALF + 1, f * STRIP + y] = table[s, k]
        for i in range(DEGREES[s] + 1 - k):
            spread_out[index[s, i, k], i, f * SPAN : (f + 1) * SPAN] = 1.0
            for x in range(STRIP):
                start = f * SPAN + x + EDGE - HALF
                rows[i, x, start : start + 2 * HALF + 1] = table[s, i]
    return columns, rows, spread_out.reshape(len(index), -1)


def mixing_kernel(coef_ref, rows_ref, out_ref):
    def mixed(q, lo, hi):
        total = None
        for i in range(POWERS):
            used = [f for f, (s, k) in enumerate(FILTERS) if i + k <= DEGREES[s]]
            if not any(f * SPAN < hi and (f + 1) * SPAN > lo for f in used):
                continue
            term = coef_ref[0, q : q + 1, i * DEPTH + lo : i * DEPTH + hi] * rows_ref[i, :, lo:hi]
            total = term if total is None else total + term
        return total

    place = lax.broadcasted_iota(jnp.int32, (STRIP, 1), 0).astype(jnp.float32)
    middle = (BLK - 1) / 2.0
    for lo in range(0, DEPTH, 256):
        hi = lo + 256
        flat, across, down = mixed(0, lo, hi), mixed(1, lo, hi), mixed(2, lo, hi)
        parts = [flat + (place + (STRIP * t - middle)) / middle * down for t in range(2)] + [across]
        for p, part in enumerate(parts):
            high, low = split(part)
            out_ref[0, p, 0, :, lo:hi] = high
            out_ref[0, p, 1, :, lo:hi] = low


def mixing(expanded, rows):
    blocks = expanded.shape[0]
    return pl.pallas_call(
        mixing_kernel,
        grid=(blocks,),
        in_specs=[
            pl.BlockSpec((1, 3, POWERS * DEPTH), lambda n: (n, 0, 0)),
            pl.BlockSpec((POWERS, STRIP, DEPTH), lambda n: (0, 0, 0)),
        ],
        out_specs=pl.BlockSpec((1, 3, 2, STRIP, DEPTH), lambda n: (n, 0, 0, 0, 0)),
        out_shape=jax.ShapeDtypeStruct((blocks, 3, 2, STRIP, DEPTH), jnp.bfloat16),
        compiler_params=pltpu.CompilerParams(vmem_limit_bytes=40 << 20),
        cost_estimate=pl.CostEstimate(
            flops=blocks * 40 * STRIP * DEPTH, bytes_accessed=blocks * 14 * STRIP * DEPTH, transcendentals=0
        ),
        name="row_matrices",
    )(expanded, rows)


def model_kernel(row_tiles, col_tiles, subs, tile_ref, place_ref, mix_ref, warped_ref, chigh_ref, clow_ref,
                 sky_ref, out_ref, window, bhigh, blow, sems):
    step = pl.program_id(0)
    steps = pl.num_programs(0)
    tile_rows = subs * BLK

    def corner(n):
        tile, place = tile_ref[n], place_ref[n]
        return (tile // col_tiles) * subs + place // subs, (tile % col_tiles) * subs + place % subs

    def copies(n, slot):
        a, b = corner(n)
        found = []
        for dr, (from_row, to_row, height) in enumerate(((BLK - EDGE, 0, EDGE), (0, EDGE, BLK), (0, EDGE + BLK, EDGE))):
            for dc, (from_col, to_col, width) in enumerate(((BLK - LANE, 0, LANE), (0, LANE, BLK), (0, LANE + BLK, LANE))):
                ra = jnp.clip(a + dr - 1, 0, row_tiles * subs - 1)
                cb = jnp.clip(b + dc - 1, 0, col_tiles * subs - 1)
                row = ((ra // subs) * col_tiles + cb // subs) * tile_rows + (ra % subs) * BLK + from_row
                col = (cb % subs) * BLK + from_col
                found.append(
                    pltpu.make_async_copy(
                        sky_ref.at[pl.ds(pl.multiple_of(row, EDGE), height), pl.ds(pl.multiple_of(col, LANE), width)],
                        window.at[slot, pl.ds(to_row, height), pl.ds(to_col, width)],
                        sems.at[slot, dr * 3 + dc],
                    )
                )
        return found

    @pl.when(step == 0)
    def _():
        used = len(FILTERS) * SPAN
        for t in range(2):
            bhigh[t, used:, :] = jnp.zeros((DEPTH - used, BLK), jnp.bfloat16)
            blow[t, used:, :] = jnp.zeros((DEPTH - used, BLK), jnp.bfloat16)
        for copy in copies(0, 0):
            copy.start()

    slot = lax.rem(step, 2)

    @pl.when(step + 1 < steps)
    def _():
        for copy in copies(step + 1, 1 - slot):
            copy.start()

    for copy in copies(step, slot):
        copy.wait()

    a, b = corner(step)
    rows_all, cols_all = BLK + 2 * EDGE, BLK + 2 * LANE

    @pl.when(a == 0)
    def _():
        window[slot, :EDGE, :] = jnp.zeros((EDGE, cols_all), jnp.float32)

    @pl.when(a == row_tiles * subs - 1)
    def _():
        window[slot, EDGE + BLK :, :] = jnp.zeros((EDGE, cols_all), jnp.float32)

    @pl.when(b == 0)
    def _():
        window[slot, :, :LANE] = jnp.zeros((rows_all, LANE), jnp.float32)

    @pl.when(b == col_tiles * subs - 1)
    def _():
        window[slot, :, LANE + BLK :] = jnp.zeros((rows_all, LANE), jnp.float32)

    dot = lambda x, y: jnp.dot(x, y, preferred_element_type=jnp.float32)
    shifted = pltpu.roll(window[slot], cols_all - (LANE - HALF), 1)
    high, low = split(shifted)
    high = jnp.concatenate([high[:, :BLK], high[:, STRIP : STRIP + BLK]], axis=0)
    low = jnp.concatenate([low[:, :BLK], low[:, STRIP : STRIP + BLK]], axis=0)
    for lo in range(0, len(FILTERS), 2):
        count = min(2, len(FILTERS) - lo)
        lanes = slice(lo * STRIP, (lo + count) * STRIP)
        chigh = chigh_ref[:, lanes]
        product = dot(high, chigh) + dot(low, chigh) + dot(high, clow_ref[:, lanes])
        phigh, plow = split(product)
        for f in range(count):
            for yt in range(2):
                for xt in range(2):
                    start = yt * rows_all + xt * STRIP
                    source = (slice(start, start + SPAN), slice(f * STRIP, (f + 1) * STRIP))
                    target = (xt, slice((lo + f) * SPAN, (lo + f + 1) * SPAN), slice(yt * STRIP, (yt + 1) * STRIP))
                    bhigh[target] = phigh[source]
                    blow[target] = plow[source]

    middle = (BLK - 1) / 2.0
    across = (lax.broadcasted_iota(jnp.int32, (1, BLK), 1).astype(jnp.float32) - middle) / middle
    for t in range(2):
        mhigh = jnp.concatenate([mix_ref[0, t, 0], mix_ref[0, 2, 0]], axis=0)
        mlow = jnp.concatenate([mix_ref[0, t, 1], mix_ref[0, 2, 1]], axis=0)
        right = bhigh[t]
        both = dot(mhigh, right) + dot(mlow, right) + dot(mhigh, blow[t])
        model = both[:STRIP] + across * both[STRIP:]
        rows = slice(t * STRIP, (t + 1) * STRIP)
        out_ref[0, rows, :] = warped_ref[0, rows, :] - model


def differences(sky, mix, warped, dest, place, row_tiles, col_tiles, subs, chigh, clow):
    blocks = warped.shape[0]
    rows_all, cols_all = BLK + 2 * EDGE, BLK + 2 * LANE

    def kernel(*refs):
        model_kernel(row_tiles, col_tiles, subs, *refs)

    return pl.pallas_call(
        kernel,
        grid_spec=pltpu.PrefetchScalarGridSpec(
            num_scalar_prefetch=2,
            grid=(blocks,),
            in_specs=[
                pl.BlockSpec((1, 3, 2, STRIP, DEPTH), lambda n, *_: (n, 0, 0, 0, 0)),
                pl.BlockSpec((1, BLK, BLK), lambda n, *_: (n, 0, 0)),
                pl.BlockSpec(chigh.shape, lambda n, *_: (0, 0)),
                pl.BlockSpec(clow.shape, lambda n, *_: (0, 0)),
                pl.BlockSpec(memory_space=pl.ANY),
            ],
            out_specs=pl.BlockSpec((1, BLK, BLK), lambda n, *_: (n, 0, 0)),
            scratch_shapes=[
                pltpu.VMEM((2, rows_all, cols_all), jnp.float32),
                pltpu.VMEM((2, DEPTH, BLK), jnp.bfloat16),
                pltpu.VMEM((2, DEPTH, BLK), jnp.bfloat16),
                pltpu.SemaphoreType.DMA((2, 9)),
            ],
        ),
        out_shape=jax.ShapeDtypeStruct(warped.shape, jnp.float32),
        compiler_params=pltpu.CompilerParams(vmem_limit_bytes=48 << 20),
        cost_estimate=pl.CostEstimate(
            flops=blocks * 2900000000, bytes_accessed=blocks * 4000000, transcendentals=0
        ),
        name="differences",
    )(dest, place, mix, warped, chigh, clow, sky)


def local_part(sky, warped, coeffs, dest, place, row_tiles, col_tiles, subs):
    columns, rows, spread_out = constants()
    chigh = columns.astype(jnp.bfloat16)
    clow = (columns - chigh.astype(np.float32)).astype(jnp.bfloat16)
    expanded = jnp.einsum("nbq,bk->nqk", coeffs, spread_out, precision=lax.Precision.HIGHEST)
    mix = mixing(expanded, jnp.asarray(rows))
    return differences(
        sky, mix, warped, dest, place, row_tiles, col_tiles, subs, jnp.asarray(chigh), jnp.asarray(clow)
    )


def gather_kernel(columns, order, own_ref, sky_ref, z_up, z_down, z_recv, f_send, f_recv, g_send, g_recv,
                  k_send, k_recv, local_sem):
    trow, tcol, visit = lax.axis_index("trow"), lax.axis_index("tcol"), lax.axis_index("visit")
    height = own_ref.shape[0]
    half = height // 2
    sibling = (trow + 1 - 2 * lax.rem(trow, 2), tcol, visit)
    across_x = (lax.rem(trow + 2, 4), tcol, visit)
    across_y = (trow, tcol, 1 - visit)
    above = (trow, tcol + 1, visit)
    below = (trow, tcol - 1, visit)
    has_above, has_below = tcol < columns - 1, tcol > 0

    barrier = pltpu.get_barrier_semaphore()

    def greet(device):
        pl.semaphore_signal(barrier, inc=1, device_id=device, device_id_type=pl.DeviceIdType.MESH)

    for device in (sibling, across_x, across_y):
        greet(device)

    @pl.when(has_above)
    def _():
        greet(above)

    @pl.when(has_below)
    def _():
        greet(below)

    pl.semaphore_wait(barrier, 3 + jnp.where(has_above, 1, 0) + jnp.where(has_below, 1, 0))

    def place(row, col, vis, h):
        start = ((row * columns + col) * 2 + vis) * height + h * half
        return sky_ref.at[pl.ds(pl.multiple_of(start, half), half), :]

    def remote(source, target, send, recv, device):
        return pltpu.make_async_remote_copy(
            src_ref=source, dst_ref=target, send_sem=send, recv_sem=recv,
            device_id=device, device_id_type=pl.DeviceIdType.MESH,
        )

    def home(h, w):
        swap_x = (w % 2 == 1) if h == 0 else (w >= 2)
        swap_y = (w >= 2) if h == 0 else (w % 2 == 1)
        return (lax.rem(trow + 2, 4) if swap_x else trow), (1 - visit if swap_y else visit)

    first = (across_x, across_y)
    second = (across_y, across_x)

    def slot(h, w, s):
        row, vis = home(h, w)
        return place(row, s, vis, h)

    def held(h, w, s, fresh):
        return own_ref.at[pl.ds(h * half, half), :] if fresh else slot(h, w, s)

    def up(h, s, fresh=False):
        return remote(held(h, 0, s, fresh), slot(h, 0, s), z_up.at[h, s], z_recv.at[h, s], above)

    def down(h, s, fresh=False):
        return remote(held(h, 0, s, fresh), slot(h, 0, s), z_down.at[h, s], z_recv.at[h, s], below)

    def one(h, s, fresh=False):
        return remote(held(h, 0, s, fresh), slot(h, 0, s), f_send.at[h, s], f_recv.at[h, s], first[h])

    def two(h, w, s, fresh=False):
        return remote(held(h, w, s, fresh), slot(h, w, s), g_send.at[h, w, s], g_recv.at[h, w, s], second[h])

    def hand(h, w, s, fresh=False):
        return remote(held(h, w, s, fresh), slot(h, w, s), k_send.at[h, w, s], k_recv.at[h, w, s], sibling)

    spots = []
    for j in range(columns):
        s = jnp.int32(0)
        for z in range(columns):
            s = jnp.where(tcol == z, order[z][j], s)
        spots.append(s)

    mine = pltpu.make_async_copy(own_ref, sky_ref.at[
        pl.ds(pl.multiple_of(((trow * columns + tcol) * 2 + visit) * height, height), height), :], local_sem)
    mine.start()

    def moves_up(s):
        return jnp.logical_and(has_above, s <= tcol)

    def moves_down(s):
        return jnp.logical_and(has_below, s >= tcol)

    def column_item(h, s, fresh):
        @pl.when(moves_up(s))
        def _():
            up(h, s, fresh).start()

        @pl.when(moves_down(s))
        def _():
            down(h, s, fresh).start()

        one(h, s, fresh).start()
        two(h, 0, s, fresh).start()
        hand(h, 0, s, fresh).start()

    def partner_item(h, s):
        one_in = remote(slot(h, 1, s), slot(h, 1, s), f_send.at[h, s], f_recv.at[h, s], first[h])
        one_in.wait_recv()
        two(h, 1, s).start()
        hand(h, 1, s).start()

    for j, s in enumerate(spots):
        for h in range(2):
            if j > 0:
                up_in = remote(slot(h, 0, s), slot(h, 0, s), z_up.at[h, s], z_recv.at[h, s], across_x)
                up_in.wait_recv()
            column_item(h, s, j == 0)
        if j > 0:
            for h in range(2):
                partner_item(h, spots[j - 1])
    for h in range(2):
        partner_item(h, spots[-1])
    for w in range(2):
        for s in spots:
            for h in range(2):
                two_in = remote(
                    slot(h, 2 + w, s), slot(h, 2 + w, s), g_send.at[h, w, s], g_recv.at[h, w, s], second[h]
                )
                two_in.wait_recv()
                hand(h, 2 + w, s).start()

    other = lax.rem(trow, 2)
    for j, s in enumerate(spots):
        for h in range(2):
            for w in range(4):
                row, vis = home(h, w)
                landed = place(row + 1 - 2 * other, s, vis, h)
                remote(landed, landed, k_send.at[h, w, s], k_recv.at[h, w, s], sibling).wait_recv()
    mine.wait()
    for j, s in enumerate(spots):
        fresh = j == 0
        for h in range(2):
            @pl.when(moves_up(s))
            def _():
                up(h, s, fresh).wait_send()

            @pl.when(moves_down(s))
            def _():
                down(h, s, fresh).wait_send()

            one(h, s, fresh).wait_send()
            for w in range(2):
                two(h, w, s, fresh and w == 0).wait_send()
            for w in range(4):
                hand(h, w, s, fresh and w == 0).wait_send()


def gathered(template, columns, devices):
    order = [sorted(range(columns), key=lambda s: (abs(s - z), s)) for z in range(columns)]
    dma = pltpu.SemaphoreType.DMA

    def kernel(*refs):
        gather_kernel(columns, order, *refs)

    return pl.pallas_call(
        kernel,
        in_specs=[pl.BlockSpec(memory_space=pl.ANY)],
        out_specs=pl.BlockSpec(memory_space=pl.ANY),
        out_shape=jax.ShapeDtypeStruct((devices * template.shape[0], template.shape[1]), template.dtype),
        scratch_shapes=[
            dma((2, columns)), dma((2, columns)), dma((2, columns)),
            dma((2, columns)), dma((2, columns)),
            dma((2, 2, columns)), dma((2, 2, columns)),
            dma((2, 4, columns)), dma((2, 4, columns)),
            dma,
        ],
        compiler_params=pltpu.CompilerParams(
            collective_id=0, has_side_effects=True, vmem_limit_bytes=60 << 20
        ),
        cost_estimate=pl.CostEstimate(
            flops=0, bytes_accessed=2 * devices * template.size * 4, transcendentals=0
        ),
        name="gather_template",
    )(template)


def on_device(template, warped, coeffs, dest_tile, position):
    axes = ("trow", "tcol", "visit")
    sizes = [lax.axis_size(axis) for axis in axes]
    if sizes[0] == 4 and sizes[2] == 2:
        sky = gathered(template, sizes[1], sizes[0] * sizes[1] * sizes[2])
    else:
        sky = lax.all_gather(template, axes, axis=0, tiled=True)
    subs = template.shape[1] // BLK
    return local_part(
        sky, warped, coeffs, dest_tile[:, 0], position[:, 0],
        lax.axis_size("trow"), lax.axis_size("tcol"), subs,
    )


def solution(mesh):
    return jax.shard_map(
        on_device,
        mesh=mesh,
        in_specs=(
            P(("trow", "visit"), "tcol"),
            P(("trow", "tcol", "visit"), None, None),
            P(("trow", "tcol", "visit"), None, None),
            P(("trow", "tcol", "visit"), None),
            P(("trow", "tcol", "visit"), None),
        ),
        out_specs=P(("trow", "tcol", "visit"), None, None),
        check_vma=False,
    )
```

```python
import jax
import jax.numpy as jnp
import numpy as np
from jax import lax
from jax.experimental import pallas as pl
from jax.experimental.pallas import tpu as pltpu
from jax.sharding import PartitionSpec as P

BLK = 256
HALF = 10
SPREADS = (1.0, 2.0, 4.0)
DEGREES = (4, 2, 2)
STRIP = 128
EDGE = 16
SPAN = STRIP + 2 * EDGE
LANE = 128
FILTERS = [(s, k) for s in range(3) for k in range(DEGREES[s] + 1)]
DEPTH = -(-len(FILTERS) * SPAN // 256) * 256
POWERS = max(DEGREES) + 1


def taps():
    offsets = np.arange(-HALF, HALF + 1).astype(np.float64)
    table = {}
    for s, spread in enumerate(SPREADS):
        for k in range(DEGREES[s] + 1):
            weights = offsets**k * np.exp(-offsets * offsets / (2.0 * spread * spread))
            table[s, k] = weights / np.sqrt(np.sum(weights * weights))
    return table


def split(values):
    high = values.astype(jnp.bfloat16)
    return high, (values - high.astype(jnp.float32)).astype(jnp.bfloat16)


def constants():
    table = taps()
    index = {}
    for s, degree in enumerate(DEGREES):
        for i in range(degree + 1):
            for j in range(degree + 1 - i):
                index[s, i, j] = len(index)
    columns = np.zeros((2 * STRIP, len(FILTERS) * STRIP), np.float32)
    rows = np.zeros((POWERS, STRIP, DEPTH), np.float32)
    spread_out = np.zeros((len(index), POWERS, DEPTH), np.float32)
    for f, (s, k) in enumerate(FILTERS):
        for y in range(STRIP):
            columns[y : y + 2 * HALF + 1, f * STRIP + y] = table[s, k]
        for i in range(DEGREES[s] + 1 - k):
            spread_out[index[s, i, k], i, f * SPAN : (f + 1) * SPAN] = 1.0
            for x in range(STRIP):
                start = f * SPAN + x + EDGE - HALF
                rows[i, x, start : start + 2 * HALF + 1] = table[s, i]
    return columns, rows, spread_out.reshape(len(index), -1)


def mixing_kernel(coef_ref, rows_ref, out_ref):
    def mixed(q, lo, hi):
        total = None
        for i in range(POWERS):
            used = [f for f, (s, k) in enumerate(FILTERS) if i + k <= DEGREES[s]]
            if not any(f * SPAN < hi and (f + 1) * SPAN > lo for f in used):
                continue
            term = coef_ref[0, q : q + 1, i * DEPTH + lo : i * DEPTH + hi] * rows_ref[i, :, lo:hi]
            total = term if total is None else total + term
        return total

    place = lax.broadcasted_iota(jnp.int32, (STRIP, 1), 0).astype(jnp.float32)
    middle = (BLK - 1) / 2.0
    for lo in range(0, DEPTH, 256):
        hi = lo + 256
        flat, across, down = mixed(0, lo, hi), mixed(1, lo, hi), mixed(2, lo, hi)
        parts = [flat + (place + (STRIP * t - middle)) / middle * down for t in range(2)] + [across]
        for p, part in enumerate(parts):
            high, low = split(part)
            out_ref[0, p, 0, :, lo:hi] = high
            out_ref[0, p, 1, :, lo:hi] = low


def mixing(expanded, rows):
    blocks = expanded.shape[0]
    return pl.pallas_call(
        mixing_kernel,
        grid=(blocks,),
        in_specs=[
            pl.BlockSpec((1, 3, POWERS * DEPTH), lambda n: (n, 0, 0)),
            pl.BlockSpec((POWERS, STRIP, DEPTH), lambda n: (0, 0, 0)),
        ],
        out_specs=pl.BlockSpec((1, 3, 2, STRIP, DEPTH), lambda n: (n, 0, 0, 0, 0)),
        out_shape=jax.ShapeDtypeStruct((blocks, 3, 2, STRIP, DEPTH), jnp.bfloat16),
        compiler_params=pltpu.CompilerParams(vmem_limit_bytes=40 << 20),
        cost_estimate=pl.CostEstimate(
            flops=blocks * 40 * STRIP * DEPTH, bytes_accessed=blocks * 14 * STRIP * DEPTH, transcendentals=0
        ),
        name="row_matrices",
    )(expanded, rows)


def model_kernel(row_tiles, col_tiles, subs, tile_ref, place_ref, mix_ref, warped_ref, chigh_ref, clow_ref,
                 sky_ref, out_ref, window, bhigh, blow, sems):
    step = pl.program_id(0)
    steps = pl.num_programs(0)
    tile_rows = subs * BLK

    def corner(n):
        tile, place = tile_ref[n], place_ref[n]
        return (tile // col_tiles) * subs + place // subs, (tile % col_tiles) * subs + place % subs

    def copies(n, slot):
        a, b = corner(n)
        found = []
        for dr, (from_row, to_row, height) in enumerate(((BLK - EDGE, 0, EDGE), (0, EDGE, BLK), (0, EDGE + BLK, EDGE))):
            for dc, (from_col, to_col, width) in enumerate(((BLK - LANE, 0, LANE), (0, LANE, BLK), (0, LANE + BLK, LANE))):
                ra = jnp.clip(a + dr - 1, 0, row_tiles * subs - 1)
                cb = jnp.clip(b + dc - 1, 0, col_tiles * subs - 1)
                row = ((ra // subs) * col_tiles + cb // subs) * tile_rows + (ra % subs) * BLK + from_row
                col = (cb % subs) * BLK + from_col
                found.append(
                    pltpu.make_async_copy(
                        sky_ref.at[pl.ds(pl.multiple_of(row, EDGE), height), pl.ds(pl.multiple_of(col, LANE), width)],
                        window.at[slot, pl.ds(to_row, height), pl.ds(to_col, width)],
                        sems.at[slot, dr * 3 + dc],
                    )
                )
        return found

    @pl.when(step == 0)
    def _():
        used = len(FILTERS) * SPAN
        for t in range(2):
            bhigh[t, used:, :] = jnp.zeros((DEPTH - used, BLK), jnp.bfloat16)
            blow[t, used:, :] = jnp.zeros((DEPTH - used, BLK), jnp.bfloat16)
        for copy in copies(0, 0):
            copy.start()

    slot = lax.rem(step, 2)

    @pl.when(step + 1 < steps)
    def _():
        for copy in copies(step + 1, 1 - slot):
            copy.start()

    for copy in copies(step, slot):
        copy.wait()

    a, b = corner(step)
    rows_all, cols_all = BLK + 2 * EDGE, BLK + 2 * LANE

    @pl.when(a == 0)
    def _():
        window[slot, :EDGE, :] = jnp.zeros((EDGE, cols_all), jnp.float32)

    @pl.when(a == row_tiles * subs - 1)
    def _():
        window[slot, EDGE + BLK :, :] = jnp.zeros((EDGE, cols_all), jnp.float32)

    @pl.when(b == 0)
    def _():
        window[slot, :, :LANE] = jnp.zeros((rows_all, LANE), jnp.float32)

    @pl.when(b == col_tiles * subs - 1)
    def _():
        window[slot, :, LANE + BLK :] = jnp.zeros((rows_all, LANE), jnp.float32)

    dot = lambda x, y: jnp.dot(x, y, preferred_element_type=jnp.float32)
    shifted = pltpu.roll(window[slot], cols_all - (LANE - HALF), 1)
    high, low = split(shifted)
    high = jnp.concatenate([high[:, :BLK], high[:, STRIP : STRIP + BLK]], axis=0)
    low = jnp.concatenate([low[:, :BLK], low[:, STRIP : STRIP + BLK]], axis=0)
    for lo in range(0, len(FILTERS), 2):
        count = min(2, len(FILTERS) - lo)
        lanes = slice(lo * STRIP, (lo + count) * STRIP)
        chigh = chigh_ref[:, lanes]
        product = dot(high, chigh) + dot(low, chigh) + dot(high, clow_ref[:, lanes])
        phigh, plow = split(product)
        for f in range(count):
            for yt in range(2):
                for xt in range(2):
                    start = yt * rows_all + xt * STRIP
                    source = (slice(start, start + SPAN), slice(f * STRIP, (f + 1) * STRIP))
                    target = (xt, slice((lo + f) * SPAN, (lo + f + 1) * SPAN), slice(yt * STRIP, (yt + 1) * STRIP))
                    bhigh[target] = phigh[source]
                    blow[target] = plow[source]

    middle = (BLK - 1) / 2.0
    across = (lax.broadcasted_iota(jnp.int32, (1, BLK), 1).astype(jnp.float32) - middle) / middle
    for t in range(2):
        mhigh = jnp.concatenate([mix_ref[0, t, 0], mix_ref[0, 2, 0]], axis=0)
        mlow = jnp.concatenate([mix_ref[0, t, 1], mix_ref[0, 2, 1]], axis=0)
        right = bhigh[t]
        both = dot(mhigh, right) + dot(mlow, right) + dot(mhigh, blow[t])
        model = both[:STRIP] + across * both[STRIP:]
        rows = slice(t * STRIP, (t + 1) * STRIP)
        out_ref[0, rows, :] = warped_ref[0, rows, :] - model


def differences(sky, mix, warped, dest, place, row_tiles, col_tiles, subs, chigh, clow):
    blocks = warped.shape[0]
    rows_all, cols_all = BLK + 2 * EDGE, BLK + 2 * LANE

    def kernel(*refs):
        model_kernel(row_tiles, col_tiles, subs, *refs)

    return pl.pallas_call(
        kernel,
        grid_spec=pltpu.PrefetchScalarGridSpec(
            num_scalar_prefetch=2,
            grid=(blocks,),
            in_specs=[
                pl.BlockSpec((1, 3, 2, STRIP, DEPTH), lambda n, *_: (n, 0, 0, 0, 0)),
                pl.BlockSpec((1, BLK, BLK), lambda n, *_: (n, 0, 0)),
                pl.BlockSpec(chigh.shape, lambda n, *_: (0, 0)),
                pl.BlockSpec(clow.shape, lambda n, *_: (0, 0)),
                pl.BlockSpec(memory_space=pl.ANY),
            ],
            out_specs=pl.BlockSpec((1, BLK, BLK), lambda n, *_: (n, 0, 0)),
            scratch_shapes=[
                pltpu.VMEM((2, rows_all, cols_all), jnp.float32),
                pltpu.VMEM((2, DEPTH, BLK), jnp.bfloat16),
                pltpu.VMEM((2, DEPTH, BLK), jnp.bfloat16),
                pltpu.SemaphoreType.DMA((2, 9)),
            ],
        ),
        out_shape=jax.ShapeDtypeStruct(warped.shape, jnp.float32),
        compiler_params=pltpu.CompilerParams(vmem_limit_bytes=48 << 20),
        cost_estimate=pl.CostEstimate(
            flops=blocks * 2900000000, bytes_accessed=blocks * 4000000, transcendentals=0
        ),
        name="differences",
    )(dest, place, mix, warped, chigh, clow, sky)


def local_part(sky, mix, warped, dest, place, row_tiles, col_tiles, subs):
    columns = constants()[0]
    chigh = columns.astype(jnp.bfloat16)
    clow = (columns - chigh.astype(np.float32)).astype(jnp.bfloat16)
    return differences(
        sky, mix, warped, dest, place, row_tiles, col_tiles, subs, jnp.asarray(chigh), jnp.asarray(clow)
    )


def gather_kernel(columns, order, own_ref, coef_ref, spread_ref, rows_ref, sky_ref, mix_ref, z_up, z_down, z_recv,
                  f_send, f_recv, g_send, g_recv, k_send, k_recv, local_sem, coef, spread, rows, expanded, stage,
                  load_sems, store_sems):
    trow, tcol, visit = lax.axis_index("trow"), lax.axis_index("tcol"), lax.axis_index("visit")
    height = own_ref.shape[0]
    half = height // 2
    sibling = (trow + 1 - 2 * lax.rem(trow, 2), tcol, visit)
    across_x = (lax.rem(trow + 2, 4), tcol, visit)
    across_y = (trow, tcol, 1 - visit)
    above = (trow, tcol + 1, visit)
    below = (trow, tcol - 1, visit)
    has_above, has_below = tcol < columns - 1, tcol > 0

    barrier = pltpu.get_barrier_semaphore()

    def greet(device):
        pl.semaphore_signal(barrier, inc=1, device_id=device, device_id_type=pl.DeviceIdType.MESH)

    for device in (sibling, across_x, across_y):
        greet(device)

    @pl.when(has_above)
    def _():
        greet(above)

    @pl.when(has_below)
    def _():
        greet(below)

    pl.semaphore_wait(barrier, 3 + jnp.where(has_above, 1, 0) + jnp.where(has_below, 1, 0))

    def place(row, col, vis, h):
        start = ((row * columns + col) * 2 + vis) * height + h * half
        return sky_ref.at[pl.ds(pl.multiple_of(start, half), half), :]

    def remote(source, target, send, recv, device):
        return pltpu.make_async_remote_copy(
            src_ref=source, dst_ref=target, send_sem=send, recv_sem=recv,
            device_id=device, device_id_type=pl.DeviceIdType.MESH,
        )

    def home(h, w):
        swap_x = (w % 2 == 1) if h == 0 else (w >= 2)
        swap_y = (w >= 2) if h == 0 else (w % 2 == 1)
        return (lax.rem(trow + 2, 4) if swap_x else trow), (1 - visit if swap_y else visit)

    first = (across_x, across_y)
    second = (across_y, across_x)

    def slot(h, w, s):
        row, vis = home(h, w)
        return place(row, s, vis, h)

    def held(h, w, s, fresh):
        return own_ref.at[pl.ds(h * half, half), :] if fresh else slot(h, w, s)

    def up(h, s, fresh=False):
        return remote(held(h, 0, s, fresh), slot(h, 0, s), z_up.at[h, s], z_recv.at[h, s], above)

    def down(h, s, fresh=False):
        return remote(held(h, 0, s, fresh), slot(h, 0, s), z_down.at[h, s], z_recv.at[h, s], below)

    def one(h, s, fresh=False):
        return remote(held(h, 0, s, fresh), slot(h, 0, s), f_send.at[h, s], f_recv.at[h, s], first[h])

    def two(h, w, s, fresh=False):
        return remote(held(h, w, s, fresh), slot(h, w, s), g_send.at[h, w, s], g_recv.at[h, w, s], second[h])

    def hand(h, w, s, fresh=False):
        return remote(held(h, w, s, fresh), slot(h, w, s), k_send.at[h, w, s], k_recv.at[h, w, s], sibling)

    spots = []
    for j in range(columns):
        s = jnp.int32(0)
        for z in range(columns):
            s = jnp.where(tcol == z, order[z][j], s)
        spots.append(s)

    mine = pltpu.make_async_copy(own_ref, sky_ref.at[
        pl.ds(pl.multiple_of(((trow * columns + tcol) * 2 + visit) * height, height), height), :], local_sem)
    mine.start()

    loads = [
        pltpu.make_async_copy(source, target, load_sems.at[k])
        for k, (source, target) in enumerate(((coef_ref, coef), (spread_ref, spread), (rows_ref, rows)))
    ]
    for load in loads:
        load.start()
    blocks = mix_ref.shape[0]
    stores = [pltpu.make_async_copy(stage.at[n % 2], mix_ref.at[n], store_sems.at[n % 2]) for n in range(blocks)]
    middle = (BLK - 1) / 2.0

    def build(n):
        if n == 0:
            for load in loads:
                load.wait()
            expanded[...] = jnp.dot(
                coef[...], spread[...], precision=lax.Precision.HIGHEST, preferred_element_type=jnp.float32
            )
        if n >= 2:
            stores[n - 2].wait()

        def chunk(c, carry):
            lo = pl.multiple_of(c * LANE, LANE)
            flat, across, down = [
                sum(
                    expanded[3 * n + q : 3 * n + q + 1, pl.ds(pl.multiple_of(i * DEPTH + lo, LANE), LANE)]
                    * rows[i, :, pl.ds(lo, LANE)]
                    for i in range(POWERS)
                )
                for q in range(3)
            ]
            place_in = lax.broadcasted_iota(jnp.int32, (STRIP, 1), 0).astype(jnp.float32)
            parts = [flat + (place_in + (STRIP * t - middle)) / middle * down for t in range(2)] + [across]
            for p, part in enumerate(parts):
                part_high, part_low = split(part)
                stage[n % 2, p, 0, :, pl.ds(lo, LANE)] = part_high
                stage[n % 2, p, 1, :, pl.ds(lo, LANE)] = part_low
            return carry

        lax.fori_loop(0, DEPTH // LANE, chunk, 0)
        stores[n].start()

    waiting = list(range(blocks))

    def build_next():
        if waiting:
            build(waiting.pop(0))

    def moves_up(s):
        return jnp.logical_and(has_above, s <= tcol)

    def moves_down(s):
        return jnp.logical_and(has_below, s >= tcol)

    def column_item(h, s, fresh):
        @pl.when(moves_up(s))
        def _():
            up(h, s, fresh).start()

        @pl.when(moves_down(s))
        def _():
            down(h, s, fresh).start()

        one(h, s, fresh).start()
        two(h, 0, s, fresh).start()
        hand(h, 0, s, fresh).start()

    def partner_item(h, s):
        one_in = remote(slot(h, 1, s), slot(h, 1, s), f_send.at[h, s], f_recv.at[h, s], first[h])
        one_in.wait_recv()
        two(h, 1, s).start()
        hand(h, 1, s).start()

    for j, s in enumerate(spots):
        for h in range(2):
            if j > 0:
                up_in = remote(slot(h, 0, s), slot(h, 0, s), z_up.at[h, s], z_recv.at[h, s], across_x)
                up_in.wait_recv()
            column_item(h, s, j == 0)
        build_next()
        if j > 0:
            for h in range(2):
                partner_item(h, spots[j - 1])
            build_next()
    for h in range(2):
        partner_item(h, spots[-1])
    build_next()
    for w in range(2):
        for s in spots:
            for h in range(2):
                two_in = remote(
                    slot(h, 2 + w, s), slot(h, 2 + w, s), g_send.at[h, w, s], g_recv.at[h, w, s], second[h]
                )
                two_in.wait_recv()
                hand(h, 2 + w, s).start()
            build_next()
    while waiting:
        build_next()

    other = lax.rem(trow, 2)
    for j, s in enumerate(spots):
        for h in range(2):
            for w in range(4):
                row, vis = home(h, w)
                landed = place(row + 1 - 2 * other, s, vis, h)
                remote(landed, landed, k_send.at[h, w, s], k_recv.at[h, w, s], sibling).wait_recv()
    mine.wait()
    for store in stores[-2:]:
        store.wait()
    for j, s in enumerate(spots):
        fresh = j == 0
        for h in range(2):
            @pl.when(moves_up(s))
            def _():
                up(h, s, fresh).wait_send()

            @pl.when(moves_down(s))
            def _():
                down(h, s, fresh).wait_send()

            one(h, s, fresh).wait_send()
            for w in range(2):
                two(h, w, s, fresh and w == 0).wait_send()
            for w in range(4):
                hand(h, w, s, fresh and w == 0).wait_send()


def gathered(template, columns, devices, coeffs, spread_out, rows):
    order = [sorted(range(columns), key=lambda s: (abs(s - z), s)) for z in range(columns)]
    dma = pltpu.SemaphoreType.DMA
    blocks = coeffs.shape[0]
    listed = coeffs.transpose(0, 2, 1).reshape(blocks * 3, -1)

    def kernel(*refs):
        gather_kernel(columns, order, *refs)

    return pl.pallas_call(
        kernel,
        in_specs=[pl.BlockSpec(memory_space=pl.ANY)] * 4,
        out_specs=[pl.BlockSpec(memory_space=pl.ANY)] * 2,
        out_shape=[
            jax.ShapeDtypeStruct((devices * template.shape[0], template.shape[1]), template.dtype),
            jax.ShapeDtypeStruct((blocks, 3, 2, STRIP, DEPTH), jnp.bfloat16),
        ],
        scratch_shapes=[
            dma((2, columns)), dma((2, columns)), dma((2, columns)),
            dma((2, columns)), dma((2, columns)),
            dma((2, 2, columns)), dma((2, 2, columns)),
            dma((2, 4, columns)), dma((2, 4, columns)),
            dma,
            pltpu.VMEM(listed.shape, jnp.float32),
            pltpu.VMEM(spread_out.shape, jnp.float32),
            pltpu.VMEM(rows.shape, jnp.float32),
            pltpu.VMEM((blocks * 3, spread_out.shape[1]), jnp.float32),
            pltpu.VMEM((2, 3, 2, STRIP, DEPTH), jnp.bfloat16),
            dma((3,)),
            dma((2,)),
        ],
        compiler_params=pltpu.CompilerParams(
            collective_id=0, has_side_effects=True, vmem_limit_bytes=60 << 20
        ),
        cost_estimate=pl.CostEstimate(
            flops=0, bytes_accessed=2 * devices * template.size * 4, transcendentals=0
        ),
        name="gather_template",
    )(template, listed, spread_out, rows)


def on_device(template, warped, coeffs, dest_tile, position):
    axes = ("trow", "tcol", "visit")
    sizes = [lax.axis_size(axis) for axis in axes]
    _, rows, spread_out = constants()
    if sizes[0] == 4 and sizes[2] == 2:
        sky, mix = gathered(
            template, sizes[1], sizes[0] * sizes[1] * sizes[2], coeffs, jnp.asarray(spread_out), jnp.asarray(rows)
        )
    else:
        sky = lax.all_gather(template, axes, axis=0, tiled=True)
        expanded = jnp.einsum("nbq,bk->nqk", coeffs, spread_out, precision=lax.Precision.HIGHEST)
        mix = mixing(expanded, jnp.asarray(rows))
    subs = template.shape[1] // BLK
    return local_part(
        sky, mix, warped, dest_tile[:, 0], position[:, 0],
        lax.axis_size("trow"), lax.axis_size("tcol"), subs,
    )


def solution(mesh):
    return jax.shard_map(
        on_device,
        mesh=mesh,
        in_specs=(
            P(("trow", "visit"), "tcol"),
            P(("trow", "tcol", "visit"), None, None),
            P(("trow", "tcol", "visit"), None, None),
            P(("trow", "tcol", "visit"), None),
            P(("trow", "tcol", "visit"), None),
        ),
        out_specs=P(("trow", "tcol", "visit"), None, None),
        check_vma=False,
    )
```
